256 devices in a mesh: replica: 4 (over y), fsdp: 64 (over z, x, core).
Axes of the slice: x: 4, y: 4, z: 8, core: 2. Of those that a mesh axis runs over, the one named last changes fastest.
Arguments:
- gradients: bfloat16 [4, 48, 1024, 1024], P('replica', None, 'fsdp'), may hold values from -6 to 6
- stat_left: float32 [128, 1024, 1024], P('fsdp', 'replica'), may hold values from -6 to 6
- stat_right: float32 [128, 1024, 1024], P('fsdp', 'replica'), may hold values from -6 to 6
- root_left: bfloat16 [128, 1024, 1024], P('fsdp', 'replica'), as said below
- root_right: bfloat16 [128, 1024, 1024], P('fsdp', None, 'replica'), as said below
- block_owner: int32 [48], replicated, may hold values from 0 to 63, as said below
- block_slot: int32 [48], replicated, may hold values from 0 to 1, as said below
Outputs:
- left_new: float32 [128, 1024, 1024], P('fsdp', 'replica')
- right_new: float32 [128, 1024, 1024], P('fsdp', 'replica')
- update: bfloat16 [48, 1024, 1024], P(None, 'fsdp', 'replica')
The draws below stay inside these ranges and needn't reach their ends.
Inputs may be any that keep to these rules, and one draw needn't show every extreme that they name: `block_owner`: some owner holds 2 blocks. `block_slot`: no two blocks share both an owner and a slot. `root_left`: given inverse fourth roots. `root_right`: given inverse fourth roots.
All inputs are finite; a program needn't handle non-finite values.
Results may differ from the reference program's by a relative error of at most 0.017.
Values may be sent and summed in bfloat16 or wider, within the bound.
No kernel may reach another device: no remote copies, remote signals or barrier semaphores. Data moves between devices by JAX's collectives and lax.ppermute only.
A program may use at most 64 MiB of HBM per device.

```python
import jax
import jax.numpy as jnp
from jax import lax

BLOCK = 1024
SLOTS = 2
NBLOCKS = 48
N_REPLICA = 4
N_FSDP = 64


def draw_pairs(key):
    total = N_FSDP * SLOTS
    order = jax.random.permutation(key, total)
    first = order[0] // SLOTS
    paired = jnp.arange(total, dtype=jnp.int32)
    ranking = jnp.zeros((total,), jnp.int32).at[order].set(jnp.arange(total, dtype=jnp.int32))
    ranking = jnp.where(paired // SLOTS == first, paired % SLOTS - SLOTS, ranking)
    chosen = jnp.argsort(ranking, stable=True)[:NBLOCKS].astype(jnp.int32)
    mixing = jax.random.permutation(jax.random.fold_in(key, 99), NBLOCKS)
    return chosen[mixing].astype(jnp.int32)


def draw_block_owner(key, part):
    chosen = draw_pairs(key)
    return (chosen // SLOTS).astype(jnp.int32)


def draw_block_slot(key, part):
    chosen = draw_pairs(key)
    return (chosen % SLOTS).astype(jnp.int32)


def root_matrix(key):
    total = N_FSDP * SLOTS
    diag_key, rest_key = jax.random.split(key)
    diagonal = jnp.exp(jax.random.uniform(diag_key, (total, BLOCK), jnp.float32, -0.7, 0.7))
    noise = jax.random.normal(rest_key, (total, BLOCK, BLOCK), jnp.float32) * 0.7
    offdiag = (noise + jnp.swapaxes(noise, 1, 2)) * (0.5 / BLOCK ** 0.5)
    eye = jnp.eye(BLOCK, dtype=jnp.float32)
    return (offdiag + eye[None, :, :] * diagonal[:, :, None]).astype(jnp.bfloat16)


def draw_root_left(key, part):
    key = jax.random.fold_in(key, 11)
    return root_matrix(key)


def draw_root_right(key, part):
    key = jax.random.fold_in(key, 23)
    return root_matrix(key)


def level_of(rng, shape, cuts, least, largest):
    gain, own = 1.0, jax.random.fold_in(rng, 6)
    for position, blocks in cuts:
        steps = jnp.exp(jax.random.uniform(jax.random.fold_in(own, position), (blocks,), jnp.float32, least / len(cuts), largest / len(cuts)))
        gain = gain * jnp.repeat(steps, shape[position] // blocks).reshape([-1 if axis == position else 1 for axis in range(len(shape))])
    return gain


def normal_values(own_key, extent, spread, bound, pieces=(), held_as=jnp.bfloat16):
    array = spread * jax.random.normal(own_key, extent, jnp.float32)
    if pieces:
        array = array * level_of(own_key, extent, pieces, -0.22, 0.18)
    return jnp.clip(array, -bound, bound).astype(held_as)


def setup_inputs(seed: int = 0) -> dict:
    streams_of = jax.random.split(jax.random.key(seed), 8)
    gradients = normal_values(streams_of[0], (N_REPLICA, NBLOCKS, BLOCK, BLOCK), 0.5, 6.0, ((0, 4), (2, 64)))
    stat_left = normal_values(streams_of[1], (N_FSDP * SLOTS, BLOCK, BLOCK), 0.5, 6.0, ((0, 64), (1, 4)), jnp.float32)
    stat_right = normal_values(streams_of[2], (N_FSDP * SLOTS, BLOCK, BLOCK), 0.5, 6.0, ((0, 64), (1, 4)), jnp.float32)
    root_left = draw_root_left(jax.random.fold_in(streams_of[7], 71), 0)
    root_right = draw_root_right(jax.random.fold_in(streams_of[7], 71), 0)
    block_owner = draw_block_owner(jax.random.fold_in(streams_of[7], 71), 0)
    block_slot = draw_block_slot(jax.random.fold_in(streams_of[7], 71), 0)
    return dict(gradients=gradients, stat_left=stat_left, stat_right=stat_right, root_left=root_left, root_right=root_right, block_owner=block_owner, block_slot=block_slot)


def reference(gradients, stat_left, stat_right, root_left, root_right, block_owner, block_slot):
    summed = jnp.sum(gradients.astype(jnp.float32), axis=0).astype(jnp.bfloat16)
    target = (block_owner * SLOTS + block_slot).astype(jnp.int32)

    def visit(carry, item):
        left, right = carry
        grad, where = item
        outer_left = jnp.dot(grad, grad.T, preferred_element_type=jnp.float32) / BLOCK
        outer_right = jnp.dot(grad.T, grad, preferred_element_type=jnp.float32) / BLOCK
        left = left.at[where].add(outer_left)
        right = right.at[where].add(outer_right)
        half = jnp.dot(grad, root_right[where], preferred_element_type=jnp.float32).astype(jnp.bfloat16)
        result = jnp.dot(root_left[where], half, preferred_element_type=jnp.float32).astype(jnp.bfloat16)
        return (left, right), result

    (left_new, right_new), update = lax.scan(visit, (stat_left, stat_right), (summed, target))
    return left_new, right_new, update
```

```python
import functools

import jax
import jax.numpy as jnp
from jax import lax
from jax.experimental import pallas as pl
from jax.experimental.pallas import tpu as pltpu
from jax.sharding import PartitionSpec as P

PLANES = 4
CORES = 2
SLOTS = 2
VMEM_LIMIT = 12 * 1024 * 1024
VMEM_WHOLE = 60 * 1024 * 1024
F32 = jnp.float32
BF16 = jnp.bfloat16
ANY = pl.BlockSpec(memory_space=pl.ANY)
VMEM = pl.BlockSpec(memory_space=pltpu.VMEM)
SMEM = pl.BlockSpec(memory_space=pltpu.SMEM)


def call(body, name, out_shape, in_specs, out_specs, scratch, flops=0, nbytes=0, vmem=VMEM_LIMIT):
    return pl.pallas_call(
        body,
        name=name,
        out_shape=out_shape,
        in_specs=in_specs,
        out_specs=out_specs,
        scratch_shapes=scratch,
        compiler_params=pltpu.CompilerParams(vmem_limit_bytes=vmem),
        cost_estimate=pl.CostEstimate(flops=flops, bytes_accessed=nbytes, transcendentals=0),
    )


def like(shape, dtype=BF16):
    return jax.ShapeDtypeStruct(shape, dtype)


def my_place():
    f = lax.axis_index("fsdp")
    return lax.axis_index("replica"), f // CORES, f % CORES


def by_plane(rank, target, g, sorted_target, order, *outs):
    count = g.shape[0]
    r, _, _ = my_place()

    @pl.loop(0, count, unroll=8)
    def _(b):
        order[rank[b]] = b
        sorted_target[rank[b]] = target[b]

    for k in range(PLANES):
        plane = (r + k) % PLANES
        for j in range(count // PLANES):
            outs[k][j] = g[order[PLANES * j + plane]]


def sum_and_place(sorted_target, _, own, one, two, three, out):
    r, _, _ = my_place()
    half = out.shape[2]
    out[...] = jnp.zeros_like(out)
    for j in range(own.shape[0]):
        chip = sorted_target[PLANES * j + r] // (CORES * SLOTS)
        total = own[j].astype(F32) + one[j].astype(F32) + two[j].astype(F32) + three[j].astype(F32)
        total = total.astype(BF16)
        for h in range(CORES):
            out[CORES * chip + h] = total[:, h * half : (h + 1) * half]


def root_halves(_, left, right, *outs):
    _, _, c = my_place()
    for i, which in enumerate((c, 1 - c)):
        for s in range(SLOTS):
            out = outs[SLOTS * i + s]
            for m in range(4):
                first = pl.multiple_of(which * 512 + 128 * m, 128)
                out[m] = left[s, :, pl.ds(first, 128)]
                first = pl.multiple_of(which * 128, 128)
                out[4 + m] = right[s, 256 * m : 256 * (m + 1), pl.ds(first, 128)]


def roots_by_plane(sorted_target, *rest):
    ins, outs, (table, sems) = rest[:4], rest[4:8], rest[8:]
    r, q, c = my_place()
    for plane in range(PLANES):
        table[plane] = 0

    @pl.loop(0, sorted_target.shape[0], unroll=8)
    def _(i):
        t = sorted_target[i]

        @pl.when(t // (CORES * SLOTS) == q)
        def _():
            table[i % PLANES] = t % (CORES * SLOTS)

    for k in range(PLANES):
        local = table[(r + k) % PLANES]
        place = jnp.where(local // SLOTS == c, 0, SLOTS) + local % SLOTS
        for i in range(2 * SLOTS):
            pl.when(place == i)(pltpu.make_async_copy(ins[i], outs[k], sems.at[k]).start)
    for k in range(PLANES):
        pltpu.make_async_copy(outs[k], outs[k], sems.at[k]).wait()


def collect(*refs):
    roots, (left, right) = refs[:PLANES], refs[PLANES:]
    for k in range(PLANES):
        for m in range(4):
            left[256 * k : 256 * (k + 1), 128 * m : 128 * (m + 1)] = roots[k][m]
            right[256 * m : 256 * (m + 1), 128 * k : 128 * (k + 1)] = roots[k][4 + m]


def together(x, y):
    return pl.pallas_call(
        lambda *_: None,
        name="together",
        out_shape=[like(x.shape), like(y.shape)],
        in_specs=[VMEM] * 2,
        out_specs=[VMEM] * 2,
        input_output_aliases={0: 0, 1: 1},
        compiler_params=pltpu.CompilerParams(vmem_limit_bytes=VMEM_LIMIT),
    )(x, y)


def block_products(s_own, s_far, l_own, l_far, r_cols, out, *rest):
    grams, half = rest[:PLANES], rest[PLANES]
    r, _, c = my_place()
    near = pl.ds(pl.multiple_of(c * 512, 512), 512)
    far = pl.ds(pl.multiple_of((1 - c) * 512, 512), 512)
    for m in range(4):
        rows = slice(256 * m, 256 * (m + 1))
        total = jnp.dot(s_own[rows, :], r_cols[near, :], preferred_element_type=F32)
        total += jnp.dot(s_far[rows, :], r_cols[far, :], preferred_element_type=F32)
        half[rows, :] = total.astype(BF16)
    for k in range(PLANES):
        rows = slice(256 * k, 256 * (k + 1))
        source = (r - k + PLANES) % PLANES
        total = jnp.dot(l_own[rows, :], half[near, :], preferred_element_type=F32)
        total += jnp.dot(l_far[rows, :], half[far, :], preferred_element_type=F32)
        total = total.astype(BF16)
        if len(out.shape) == 3:
            out[pl.ds(16 * source, 16)] = total.reshape(16, 16, 512)
        else:
            for kk in range(PLANES):
                plane = (r - kk + PLANES) % PLANES
                part = total[:, 128 * kk : 128 * (kk + 1)].reshape(16, 16, 128)
                out[plane, pl.ds(16 * source, 16)] = part

    across_rows = (((1,), (1,)), ((), ()))
    across_columns = (((0,), (0,)), ((), ()))
    for k in range(PLANES):
        plane = (r + k) % PLANES
        rows = pl.ds(pl.multiple_of(plane * 256, 256), 256)
        left = lax.dot_general(s_own[rows, :], s_own[near, :], across_rows, preferred_element_type=F32)
        left += lax.dot_general(s_far[rows, :], s_far[near, :], across_rows, preferred_element_type=F32)
        grams[k][0] = (left / 1024).astype(BF16)
        columns = pl.ds(pl.multiple_of((plane % 2) * 256, 256), 256)
        strip = jnp.where(plane // 2 == c, s_own[:, columns], s_far[:, columns])
        right = lax.dot_general(strip, s_own[...], across_columns, preferred_element_type=F32)
        grams[k][1] = (right / 1024).astype(BF16)


def statistics(sorted_target, stat_left, stat_right, *rest):
    own, other, (left_new, right_new), scratch = rest[:4], rest[4:8], rest[8:10], rest[10:]
    table, added, left, right, g_sems, in_sems, out_sems = scratch
    r, q, c = my_place()
    pairs = ((stat_left, left, left_new), (stat_right, right, right_new))
    for s in range(SLOTS):
        for i, (source, here, _) in enumerate(pairs):
            pltpu.make_async_copy(source.at[s], here.at[s], in_sems.at[2 * s + i]).start()
    for s in range(SLOTS):
        table[s] = 0
        table[SLOTS + s] = 0

    @pl.loop(0, sorted_target.shape[0], unroll=8)
    def _(i):
        t = sorted_target[i]

        @pl.when(t // SLOTS == CORES * q + c)
        def _():
            table[t % SLOTS] = i % PLANES
            table[SLOTS + t % SLOTS] = 1

    near = pl.ds(pl.multiple_of(c * 512, 512), 512)
    far = pl.ds(pl.multiple_of((1 - c) * 512, 512), 512)
    for s in range(SLOTS):
        step = (r - table[s] + PLANES) % PLANES
        for k in range(PLANES):

            @pl.when(step == k)
            def _():
                pltpu.make_async_copy(own[k], added.at[s, :, :, near], g_sems.at[s]).start()
                pltpu.make_async_copy(other[k], added.at[s, :, :, far], g_sems.at[s]).start()

    stores = []
    for s in range(SLOTS):
        pltpu.make_async_copy(added.at[s], added.at[s], g_sems.at[s]).wait()
        used = table[SLOTS + s] > 0
        for i, (source, here, out) in enumerate(pairs):
            pltpu.make_async_copy(source.at[s], here.at[s], in_sems.at[2 * s + i]).wait()

            @pl.when(used)
            def _():
                here[s] = here[s] + added[s, i].astype(F32)

            store = pltpu.make_async_copy(here.at[s], out.at[s], out_sems.at[2 * s + i])
            store.start()
            stores.append(store)
    for store in stores:
        store.wait()


def pick(order, sorted_target, received, out):
    for i in range(out.shape[0]):
        chip = sorted_target[i] // (CORES * SLOTS)
        for h in range(CORES):
            out[order[i], :, 128 * h : 128 * (h + 1)] = received[i % PLANES, chip, h]


def per_device(gradients, stat_left, stat_right, root_left, root_right, block_owner, block_slot):
    blocks, rows, width = gradients.shape[1:]
    each = blocks // PLANES
    fsdp_count = lax.axis_size("fsdp")
    target = block_owner * SLOTS + block_slot
    rank = jnp.sum((target[None, :] < target[:, None]).astype(jnp.int32), axis=1)

    def along(x, step):
        return lax.ppermute(x, "replica", [(i, (i + step) % PLANES) for i in range(PLANES)])

    def across(x):
        return lax.ppermute(x, "fsdp", [(i, i ^ 1) for i in range(fsdp_count)])

    sorted_target, order, *terms = call(
        by_plane,
        "by_plane",
        [like((blocks,), jnp.int32)] * 2 + [like((each, rows, width))] * PLANES,
        [SMEM, SMEM, VMEM],
        [SMEM] * 2 + [VMEM] * PLANES,
        [],
        nbytes=3 << 20,
    )(rank, target, gradients[0])
    summands = [terms[0]] + [along(terms[k], k) for k in range(1, PLANES)]
    part = like((8, 256, 128))
    halves = call(
        root_halves,
        "root_halves",
        [part] * 4,
        [SMEM, VMEM, VMEM],
        [VMEM] * 4,
        [],
    )(sorted_target, root_left, root_right)
    halves = [*halves[:2], *(across(x) for x in halves[2:])]
    roots = call(
        roots_by_plane,
        "roots_by_plane",
        [part] * PLANES,
        [SMEM] + [VMEM] * 4,
        [VMEM] * PLANES,
        [pltpu.SMEM((PLANES,), jnp.int32), pltpu.SemaphoreType.DMA((PLANES,))],
    )(sorted_target, *halves)

    outgoing = call(
        sum_and_place,
        "sum_and_place",
        like((fsdp_count, rows, width // CORES)),
        [SMEM, ANY] + [VMEM] * PLANES,
        VMEM,
        [],
        nbytes=3 << 20,
    )(sorted_target, roots[0], *summands)
    roots, _ = lax.optimization_barrier((roots, outgoing))
    arrived = lax.all_to_all(outgoing, "fsdp", split_axis=0, concat_axis=0, tiled=True)

    roots = [roots[0]] + [along(roots[k], k) for k in range(1, PLANES)]
    l_own, r_cols = call(
        collect,
        "collect",
        [like((width, 512))] * 2,
        [VMEM] * PLANES,
        [VMEM] * 2,
        [],
    )(*roots)

    arrived, l_far = together(arrived, across(l_own))
    s_own = arrived.reshape(width, width // CORES)
    update, *grams = call(
        block_products,
        "block_products",
        [like((PLANES, fsdp_count, rows, 128))] + [like((2, 256, 512))] * PLANES,
        [VMEM] * 5,
        [VMEM] * (1 + PLANES),
        [pltpu.VMEM((width, 512), BF16)],
        flops=8 * 1024 * 1024 * 512,
        nbytes=8 << 20,
    )(s_own, across(s_own), l_own, l_far, r_cols)
    update = update.reshape(PLANES * fsdp_count, rows, 128)
    returned = lax.all_to_all(update, ("replica", "fsdp"), split_axis=0, concat_axis=0, tiled=True)
    new = call(
        pick,
        "pick",
        like((blocks, rows, width // PLANES)),
        [SMEM, SMEM, VMEM],
        VMEM,
        [],
        nbytes=2 << 20,
    )(order, sorted_target, returned.reshape(PLANES, fsdp_count // CORES, CORES, rows, 128))

    grams = [grams[0]] + [along(grams[k], k) for k in range(1, PLANES)]
    grams_far = [across(x) for x in grams]
    left_new, right_new = call(
        statistics,
        "statistics",
        [like(stat_left.shape, F32)] * 2,
        [SMEM] + [ANY] * (2 + 2 * PLANES),
        [ANY] * 2,
        [
            pltpu.SMEM((2 * SLOTS,), jnp.int32),
            pltpu.VMEM((SLOTS, 2, 256, width), BF16),
            pltpu.VMEM(stat_left.shape, F32),
            pltpu.VMEM(stat_right.shape, F32),
            pltpu.SemaphoreType.DMA((SLOTS,)),
            pltpu.SemaphoreType.DMA((2 * SLOTS,)),
            pltpu.SemaphoreType.DMA((2 * SLOTS,)),
        ],
        flops=15 * 1000**3,
        nbytes=8 << 20,
        vmem=VMEM_WHOLE,
    )(sorted_target, stat_left, stat_right, *grams, *grams_far)

    return (left_new, right_new, new)


def solution(mesh):
    placed = (
        P("replica", None, "fsdp", None),
        P("fsdp", "replica", None),
        P("fsdp", "replica", None),
        P("fsdp", "replica", None),
        P("fsdp", None, "replica"),
        P(),
        P(),
    )
    return jax.shard_map(
        per_device,
        mesh=mesh,
        in_specs=placed,
        out_specs=(
            P("fsdp", "replica", None),
            P("fsdp", "replica", None),
            P(None, "fsdp", "replica"),
        ),
        check_vma=False,
    )
```

```python
import functools

import jax
import jax.numpy as jnp
from jax import lax
from jax.experimental import pallas as pl
from jax.experimental.pallas import tpu as pltpu
from jax.sharding import PartitionSpec as P

PLANES = 4
CORES = 2
SLOTS = 2
VMEM_LIMIT = 12 * 1024 * 1024
VMEM_WHOLE = 60 * 1024 * 1024
SUM_HINT = 20 * 1000**3
ROOT_HINT = 20 * 1000**3
GRAM_HINT = 20 * 1000**3
F32 = jnp.float32
BF16 = jnp.bfloat16
ANY = pl.BlockSpec(memory_space=pl.ANY)
VMEM = pl.BlockSpec(memory_space=pltpu.VMEM)
SMEM = pl.BlockSpec(memory_space=pltpu.SMEM)


def call(body, name, out_shape, in_specs, out_specs, scratch, flops=0, nbytes=0, vmem=VMEM_LIMIT):
    return pl.pallas_call(
        body,
        name=name,
        out_shape=out_shape,
        in_specs=in_specs,
        out_specs=out_specs,
        scratch_shapes=scratch,
        compiler_params=pltpu.CompilerParams(vmem_limit_bytes=vmem),
        cost_estimate=pl.CostEstimate(flops=flops, bytes_accessed=nbytes, transcendentals=0),
    )


def like(shape, dtype=BF16):
    return jax.ShapeDtypeStruct(shape, dtype)


def my_place():
    f = lax.axis_index("fsdp")
    return lax.axis_index("replica"), f // CORES, f % CORES


def by_plane(rank, target, g, sorted_target, order, *outs):
    count = g.shape[0]
    r, _, _ = my_place()

    @pl.loop(0, count, unroll=8)
    def _(b):
        order[rank[b]] = b
        sorted_target[rank[b]] = target[b]

    for k in range(PLANES):
        plane = (r + k) % PLANES
        for j in range(count // PLANES):
            outs[k][j] = g[order[PLANES * j + plane]]


def sum_and_place(sorted_target, _, own, one, two, three, out):
    r, _, _ = my_place()
    half = out.shape[2]
    out[...] = jnp.zeros_like(out)
    for j in range(own.shape[0]):
        chip = sorted_target[PLANES * j + r] // (CORES * SLOTS)
        total = own[j].astype(F32) + one[j].astype(F32) + two[j].astype(F32) + three[j].astype(F32)
        total = total.astype(BF16)
        for h in range(CORES):
            out[CORES * chip + h] = total[:, h * half : (h + 1) * half]


def root_halves(sorted_target, left, right, *outs):
    *outs, table, slots = outs
    r, q, c = my_place()
    for i in range(8):
        table[i] = 0
    for plane in range(PLANES):
        slots[plane] = SLOTS * c

    @pl.loop(0, sorted_target.shape[0], unroll=8)
    def _(i):
        t = sorted_target[i]

        @pl.when(t // (CORES * SLOTS) == q)
        def _():
            slots[i % PLANES] = t % (CORES * SLOTS)

        @pl.when(t // SLOTS == CORES * q + c)
        def _():
            table[4 + t % SLOTS] = i % PLANES
            table[6 + t % SLOTS] = 1

    for k in range(PLANES):
        local = slots[(r + k) % PLANES]
        table[k] = jnp.where(local // SLOTS == c, 0, SLOTS) + local % SLOTS
    for i, which in enumerate((c, 1 - c)):
        for s in range(SLOTS):
            out = outs[SLOTS * i + s]
            for m in range(4):
                first = pl.multiple_of(which * 512 + 128 * m, 128)
                out[m] = left[s, :, pl.ds(first, 128)]
                first = pl.multiple_of(which * 128, 128)
                out[4 + m] = right[s, 256 * m : 256 * (m + 1), pl.ds(first, 128)]


def roots_by_plane(table, *refs):
    ins, outs = refs[:4], refs[4:]
    for k in (2, 1, 3, 0):
        for i in range(2 * SLOTS):

            @pl.when(table[k] == i)
            def _():
                outs[k][...] = ins[i][...]


def collect(*refs):
    roots, (left, right) = refs[:PLANES], refs[PLANES:]
    for k in range(PLANES):
        for m in range(4):
            left[256 * k : 256 * (k + 1), 128 * m : 128 * (m + 1)] = roots[k][m]
            right[256 * m : 256 * (m + 1), 128 * k : 128 * (k + 1)] = roots[k][4 + m]


def settle(x, flops):
    return pl.pallas_call(
        lambda *_: None,
        name="settle",
        out_shape=like(x.shape),
        in_specs=[VMEM],
        out_specs=VMEM,
        input_output_aliases={0: 0},
        compiler_params=pltpu.CompilerParams(vmem_limit_bytes=VMEM_LIMIT),
        cost_estimate=pl.CostEstimate(flops=flops, bytes_accessed=0, transcendentals=0),
    )(x)


def together(x, y):
    return pl.pallas_call(
        lambda *_: None,
        name="together",
        out_shape=[like(x.shape), like(y.shape)],
        in_specs=[VMEM] * 2,
        out_specs=[VMEM] * 2,
        input_output_aliases={0: 0, 1: 1},
        compiler_params=pltpu.CompilerParams(vmem_limit_bytes=VMEM_LIMIT),
    )(x, y)


def update_block(s_own, s_far, l_own, l_far, r_cols, out, half):
    r, _, c = my_place()
    near = pl.ds(pl.multiple_of(c * 512, 512), 512)
    far = pl.ds(pl.multiple_of((1 - c) * 512, 512), 512)
    for m in range(4):
        rows = slice(256 * m, 256 * (m + 1))
        total = jnp.dot(s_own[rows, :], r_cols[near, :], preferred_element_type=F32)
        total += jnp.dot(s_far[rows, :], r_cols[far, :], preferred_element_type=F32)
        half[rows, :] = total.astype(BF16)
    for k in range(PLANES):
        rows = slice(256 * k, 256 * (k + 1))
        source = (r - k + PLANES) % PLANES
        total = jnp.dot(l_own[rows, :], half[near, :], preferred_element_type=F32)
        total += jnp.dot(l_far[rows, :], half[far, :], preferred_element_type=F32)
        total = total.astype(BF16)
        if len(out.shape) == 3:
            out[pl.ds(16 * source, 16)] = total.reshape(16, 16, 512)
        else:
            for kk in range(PLANES):
                plane = (r - kk + PLANES) % PLANES
                part = total[:, 128 * kk : 128 * (kk + 1)].reshape(16, 16, 128)
                out[plane, pl.ds(16 * source, 16)] = part


def gram(s_own, s_far, *grams):
    r, _, c = my_place()
    near = pl.ds(pl.multiple_of(c * 512, 512), 512)
    across_rows = (((1,), (1,)), ((), ()))
    across_columns = (((0,), (0,)), ((), ()))
    for k in range(PLANES):
        plane = (r + k) % PLANES
        rows = pl.ds(pl.multiple_of(plane * 256, 256), 256)
        left = lax.dot_general(s_own[rows, :], s_own[near, :], across_rows, preferred_element_type=F32)
        left += lax.dot_general(s_far[rows, :], s_far[near, :], across_rows, preferred_element_type=F32)
        grams[k][0] = (left / 1024).astype(BF16)
        columns = pl.ds(pl.multiple_of((plane % 2) * 256, 256), 256)
        strip = jnp.where(plane // 2 == c, s_own[:, columns], s_far[:, columns])
        right = lax.dot_general(strip, s_own[...], across_columns, preferred_element_type=F32)
        grams[k][1] = (right / 1024).astype(BF16)


def statistics(table, stat_left, stat_right, *rest):
    own, other, (left_new, right_new), scratch = rest[:4], rest[4:8], rest[8:10], rest[10:]
    added, left, right, g_sems, in_sems, out_sems = scratch
    r, _, c = my_place()
    pairs = ((stat_left, left, left_new), (stat_right, right, right_new))
    near = pl.ds(pl.multiple_of(c * 512, 512), 512)
    far = pl.ds(pl.multiple_of((1 - c) * 512, 512), 512)
    for s in range(SLOTS):
        for i, (source, here, _) in enumerate(pairs):
            pltpu.make_async_copy(source.at[s], here.at[s], in_sems.at[2 * s + i]).start()
        step = (r - table[4 + s] + PLANES) % PLANES
        for k in range(PLANES):

            @pl.when(step == k)
            def _():
                pltpu.make_async_copy(own[k], added.at[s, :, :, near], g_sems.at[s]).start()
                pltpu.make_async_copy(other[k], added.at[s, :, :, far], g_sems.at[s]).start()

    stores = []
    for s in range(SLOTS):
        pltpu.make_async_copy(added.at[s], added.at[s], g_sems.at[s]).wait()
        used = table[6 + s] > 0
        for i, (source, here, out) in enumerate(pairs):
            pltpu.make_async_copy(source.at[s], here.at[s], in_sems.at[2 * s + i]).wait()

            @pl.when(used)
            def _():
                here[s] = here[s] + added[s, i].astype(F32)

            store = pltpu.make_async_copy(here.at[s], out.at[s], out_sems.at[2 * s + i])
            store.start()
            stores.append(store)
    for store in stores:
        store.wait()


def pick(order, sorted_target, received, out):
    for i in range(out.shape[0]):
        chip = sorted_target[i] // (CORES * SLOTS)
        for h in range(CORES):
            out[order[i], :, 128 * h : 128 * (h + 1)] = received[i % PLANES, chip, h]


def per_device(gradients, stat_left, stat_right, root_left, root_right, block_owner, block_slot):
    blocks, rows, width = gradients.shape[1:]
    each = blocks // PLANES
    fsdp_count = lax.axis_size("fsdp")
    target = block_owner * SLOTS + block_slot
    rank = jnp.sum((target[None, :] < target[:, None]).astype(jnp.int32), axis=1)

    def along(x, step):
        return lax.ppermute(x, "replica", [(i, (i + step) % PLANES) for i in range(PLANES)])

    def across(x):
        return lax.ppermute(x, "fsdp", [(i, i ^ 1) for i in range(fsdp_count)])

    sorted_target, order, *terms = call(
        by_plane,
        "by_plane",
        [like((blocks,), jnp.int32)] * 2 + [like((each, rows, width))] * PLANES,
        [SMEM, SMEM, VMEM],
        [SMEM] * 2 + [VMEM] * PLANES,
        [],
        nbytes=3 << 20,
    )(rank, target, gradients[0])
    summands = [terms[0]] + [settle(along(terms[k], k), SUM_HINT) for k in (1, 3, 2)]
    part = like((8, 256, 128))
    *halves, table = call(
        root_halves,
        "root_halves",
        [part] * 4 + [like((8,), jnp.int32)],
        [SMEM, VMEM, VMEM],
        [VMEM] * 4 + [SMEM],
        [pltpu.SMEM((PLANES,), jnp.int32)],
    )(sorted_target, root_left, root_right)
    halves = [*halves[:2], *(across(x) for x in halves[2:])]
    roots = call(
        roots_by_plane,
        "roots_by_plane",
        [part] * PLANES,
        [SMEM] + [VMEM] * 4,
        [VMEM] * PLANES,
        [],
    )(table, *halves)

    outgoing = call(
        sum_and_place,
        "sum_and_place",
        like((fsdp_count, rows, width // CORES)),
        [SMEM, ANY] + [VMEM] * PLANES,
        VMEM,
        [],
        nbytes=3 << 20,
    )(sorted_target, roots[0], *summands)
    roots, _ = lax.optimization_barrier((roots, outgoing))
    first = settle(along(roots[2], 2), ROOT_HINT)
    arrived = lax.all_to_all(outgoing, "fsdp", split_axis=0, concat_axis=0, tiled=True)

    roots = [roots[0], along(roots[1], 1), first, along(roots[3], 3)]
    l_own, r_cols = call(
        collect,
        "collect",
        [like((width, 512))] * 2,
        [VMEM] * PLANES,
        [VMEM] * 2,
        [],
    )(*roots)

    arrived, l_far = together(arrived, across(l_own))
    s_own = arrived.reshape(width, width // CORES)
    s_far = across(s_own)
    grams = call(
        gram,
        "gram",
        [like((2, 256, 512))] * PLANES,
        [VMEM] * 2,
        [VMEM] * PLANES,
        [],
        flops=4 * 1024 * 1024 * 512,
        nbytes=4 << 20,
    )(s_own, s_far)
    update = call(
        update_block,
        "update_block",
        like((PLANES, fsdp_count, rows, 128)),
        [VMEM] * 5,
        VMEM,
        [pltpu.VMEM((width, 512), BF16)],
        flops=4 * 1024 * 1024 * 512,
        nbytes=6 << 20,
    )(s_own, s_far, l_own, l_far, r_cols)
    update = update.reshape(PLANES * fsdp_count, rows, 128)
    returned = lax.all_to_all(update, ("replica", "fsdp"), split_axis=0, concat_axis=0, tiled=True)
    new = call(
        pick,
        "pick",
        like((blocks, rows, width // PLANES)),
        [SMEM, SMEM, VMEM],
        VMEM,
        [],
        nbytes=2 << 20,
    )(order, sorted_target, returned.reshape(PLANES, fsdp_count // CORES, CORES, rows, 128))

    grams = [grams[0]] + [along(grams[k], k) for k in range(1, PLANES)]
    grams_far = [across(x) for x in grams]
    left_new, right_new = call(
        statistics,
        "statistics",
        [like(stat_left.shape, F32)] * 2,
        [SMEM] + [ANY] * (2 + 2 * PLANES),
        [ANY] * 2,
        [
            pltpu.VMEM((SLOTS, 2, 256, width), BF16),
            pltpu.VMEM(stat_left.shape, F32),
            pltpu.VMEM(stat_right.shape, F32),
            pltpu.SemaphoreType.DMA((SLOTS,)),
            pltpu.SemaphoreType.DMA((2 * SLOTS,)),
            pltpu.SemaphoreType.DMA((2 * SLOTS,)),
        ],
        flops=15 * 1000**3,
        nbytes=8 << 20,
        vmem=VMEM_WHOLE,
    )(table, stat_left, stat_right, *grams, *grams_far)

    return (left_new, right_new, new)


def solution(mesh):
    placed = (
        P("replica", None, "fsdp", None),
        P("fsdp", "replica", None),
        P("fsdp", "replica", None),
        P("fsdp", "replica", None),
        P("fsdp", None, "replica"),
        P(),
        P(),
    )
    return jax.shard_map(
        per_device,
        mesh=mesh,
        in_specs=placed,
        out_specs=(
            P("fsdp", "replica", None),
            P("fsdp", "replica", None),
            P(None, "fsdp", "replica"),
        ),
        check_vma=False,
    )
```

```python
import functools

import jax
import jax.numpy as jnp
from jax import lax
from jax.experimental import pallas as pl
from jax.experimental.pallas import tpu as pltpu
from jax.sharding import PartitionSpec as P

PLANES = 4
CORES = 2
SLOTS = 2
VMEM_LIMIT = 12 * 1024 * 1024
VMEM_WHOLE = 60 * 1024 * 1024
SUM_HINT = 20 * 1000**3
ROOT_HINT = 20 * 1000**3
GRAM_HINT = 20 * 1000**3
F32 = jnp.float32
BF16 = jnp.bfloat16
ANY = pl.BlockSpec(memory_space=pl.ANY)
VMEM = pl.BlockSpec(memory_space=pltpu.VMEM)
SMEM = pl.BlockSpec(memory_space=pltpu.SMEM)


def call(body, name, out_shape, in_specs, out_specs, scratch, flops=0, nbytes=0, vmem=VMEM_LIMIT):
    return pl.pallas_call(
        body,
        name=name,
        out_shape=out_shape,
        in_specs=in_specs,
        out_specs=out_specs,
        scratch_shapes=scratch,
        compiler_params=pltpu.CompilerParams(vmem_limit_bytes=vmem),
        cost_estimate=pl.CostEstimate(flops=flops, bytes_accessed=nbytes, transcendentals=0),
    )


def like(shape, dtype=BF16):
    return jax.ShapeDtypeStruct(shape, dtype)


def my_place():
    f = lax.axis_index("fsdp")
    return lax.axis_index("replica"), f // CORES, f % CORES


def by_plane(rank, target, g, sorted_target, order, *outs):
    count = g.shape[0]
    r, _, _ = my_place()

    @pl.loop(0, count, unroll=8)
    def _(b):
        order[rank[b]] = b
        sorted_target[rank[b]] = target[b]

    for k in range(PLANES):
        plane = (r + k) % PLANES
        for j in range(count // PLANES):
            outs[k][j] = g[order[PLANES * j + plane]]


def sum_and_place(sorted_target, _, own, one, two, three, out):
    r, _, _ = my_place()
    half = out.shape[2]
    out[...] = jnp.zeros_like(out)
    for j in range(own.shape[0]):
        chip = sorted_target[PLANES * j + r] // (CORES * SLOTS)
        total = own[j].astype(F32) + one[j].astype(F32) + two[j].astype(F32) + three[j].astype(F32)
        total = total.astype(BF16)
        for h in range(CORES):
            out[CORES * chip + h] = total[:, h * half : (h + 1) * half]


def root_halves(sorted_target, left, right, *outs):
    *outs, table, slots = outs
    r, q, c = my_place()
    for i in range(8):
        table[i] = 0
    for plane in range(PLANES):
        slots[plane] = SLOTS * c

    @pl.loop(0, sorted_target.shape[0], unroll=8)
    def _(i):
        t = sorted_target[i]

        @pl.when(t // (CORES * SLOTS) == q)
        def _():
            slots[i % PLANES] = t % (CORES * SLOTS)

        @pl.when(t // SLOTS == CORES * q + c)
        def _():
            table[4 + t % SLOTS] = i % PLANES
            table[6 + t % SLOTS] = 1

    for k in range(PLANES):
        local = slots[(r + k) % PLANES]
        table[k] = jnp.where(local // SLOTS == c, 0, SLOTS) + local % SLOTS
    for i, which in enumerate((c, 1 - c)):
        for s in range(SLOTS):
            out = outs[SLOTS * i + s]
            for m in range(4):
                first = pl.multiple_of(which * 512 + 128 * m, 128)
                out[m] = left[s, :, pl.ds(first, 128)]
                first = pl.multiple_of(which * 128, 128)
                out[4 + m] = right[s, 256 * m : 256 * (m + 1), pl.ds(first, 128)]


def roots_by_plane(table, *refs):
    ins, outs = refs[:4], refs[4:]
    for k in (2, 1, 3, 0):
        for i in range(2 * SLOTS):

            @pl.when(table[k] == i)
            def _():
                outs[k][...] = ins[i][...]


def collect(*refs):
    roots, (left, right) = refs[:PLANES], refs[PLANES:]
    for k in range(PLANES):
        for m in range(4):
            left[256 * k : 256 * (k + 1), 128 * m : 128 * (m + 1)] = roots[k][m]
            right[256 * m : 256 * (m + 1), 128 * k : 128 * (k + 1)] = roots[k][4 + m]


def settle(x, flops):
    return pl.pallas_call(
        lambda *_: None,
        name="settle",
        out_shape=like(x.shape),
        in_specs=[VMEM],
        out_specs=VMEM,
        input_output_aliases={0: 0},
        compiler_params=pltpu.CompilerParams(vmem_limit_bytes=VMEM_LIMIT),
        cost_estimate=pl.CostEstimate(flops=flops, bytes_accessed=0, transcendentals=0),
    )(x)


def together(x, y):
    return pl.pallas_call(
        lambda *_: None,
        name="together",
        out_shape=[like(x.shape), like(y.shape)],
        in_specs=[VMEM] * 2,
        out_specs=[VMEM] * 2,
        input_output_aliases={0: 0, 1: 1},
        compiler_params=pltpu.CompilerParams(vmem_limit_bytes=VMEM_LIMIT),
    )(x, y)


def update_block(s_own, s_far, l_own, l_far, r_cols, out, half):
    r, _, c = my_place()
    near = pl.ds(pl.multiple_of(c * 512, 512), 512)
    far = pl.ds(pl.multiple_of((1 - c) * 512, 512), 512)
    for m in range(4):
        rows = slice(256 * m, 256 * (m + 1))
        total = jnp.dot(s_own[rows, :], r_cols[near, :], preferred_element_type=F32)
        total += jnp.dot(s_far[rows, :], r_cols[far, :], preferred_element_type=F32)
        half[rows, :] = total.astype(BF16)
    for k in range(PLANES):
        rows = slice(256 * k, 256 * (k + 1))
        source = (r - k + PLANES) % PLANES
        total = jnp.dot(l_own[rows, :], half[near, :], preferred_element_type=F32)
        total += jnp.dot(l_far[rows, :], half[far, :], preferred_element_type=F32)
        total = total.astype(BF16)
        if len(out.shape) == 3:
            out[pl.ds(16 * source, 16)] = total.reshape(16, 16, 512)
        else:
            for kk in range(PLANES):
                plane = (r - kk + PLANES) % PLANES
                part = total[:, 128 * kk : 128 * (kk + 1)].reshape(16, 16, 128)
                out[plane, pl.ds(16 * source, 16)] = part


def gram(s_own, s_far, *grams):
    r, _, c = my_place()
    near = pl.ds(pl.multiple_of(c * 512, 512), 512)
    across_rows = (((1,), (1,)), ((), ()))
    across_columns = (((0,), (0,)), ((), ()))
    for k in range(PLANES):
        plane = (r + k) % PLANES
        rows = pl.ds(pl.multiple_of(plane * 256, 256), 256)
        left = lax.dot_general(s_own[rows, :], s_own[near, :], across_rows, preferred_element_type=F32)
        left += lax.dot_general(s_far[rows, :], s_far[near, :], across_rows, preferred_element_type=F32)
        grams[k][0] = (left / 1024).astype(BF16)
        columns = pl.ds(pl.multiple_of((plane % 2) * 256, 256), 256)
        strip = jnp.where(plane // 2 == c, s_own[:, columns], s_far[:, columns])
        right = lax.dot_general(strip, s_own[...], across_columns, preferred_element_type=F32)
        grams[k][1] = (right / 1024).astype(BF16)


def preload(_, stat_left, stat_right, left, right, sems):
    copies = [pltpu.make_async_copy(stat_left, left, sems.at[0])]
    copies.append(pltpu.make_async_copy(stat_right, right, sems.at[1]))
    for copy in copies:
        copy.start()
    for copy in copies:
        copy.wait()


def statistics(table, left, right, *rest):
    own, other, (left_new, right_new), scratch = rest[:4], rest[4:8], rest[8:10], rest[10:]
    added, sums, g_sems, out_sems = scratch
    r, _, c = my_place()
    pairs = ((left, left_new), (right, right_new))
    near = pl.ds(pl.multiple_of(c * 512, 512), 512)
    far = pl.ds(pl.multiple_of((1 - c) * 512, 512), 512)
    for s in range(SLOTS):
        step = (r - table[4 + s] + PLANES) % PLANES
        for k in range(PLANES):

            @pl.when(step == k)
            def _():
                pltpu.make_async_copy(own[k], added.at[s, :, :, near], g_sems.at[s]).start()
                pltpu.make_async_copy(other[k], added.at[s, :, :, far], g_sems.at[s]).start()

    stores = []
    for s in range(SLOTS):
        pltpu.make_async_copy(added.at[s], added.at[s], g_sems.at[s]).wait()
        used = table[6 + s] > 0
        for i, (here, out) in enumerate(pairs):
            sums[s, i] = jnp.where(used, here[s] + added[s, i].astype(F32), here[s])
            store = pltpu.make_async_copy(sums.at[s, i], out.at[s], out_sems.at[2 * s + i])
            store.start()
            stores.append(store)
    for store in stores:
        store.wait()


def pick(order, sorted_target, received, out):
    for i in range(out.shape[0]):
        chip = sorted_target[i] // (CORES * SLOTS)
        for h in range(CORES):
            out[order[i], :, 128 * h : 128 * (h + 1)] = received[i % PLANES, chip, h]


def per_device(gradients, stat_left, stat_right, root_left, root_right, block_owner, block_slot):
    blocks, rows, width = gradients.shape[1:]
    each = blocks // PLANES
    fsdp_count = lax.axis_size("fsdp")
    target = block_owner * SLOTS + block_slot
    rank = jnp.sum((target[None, :] < target[:, None]).astype(jnp.int32), axis=1)

    def along(x, step):
        return lax.ppermute(x, "replica", [(i, (i + step) % PLANES) for i in range(PLANES)])

    def across(x):
        return lax.ppermute(x, "fsdp", [(i, i ^ 1) for i in range(fsdp_count)])

    sorted_target, order, *terms = call(
        by_plane,
        "by_plane",
        [like((blocks,), jnp.int32)] * 2 + [like((each, rows, width))] * PLANES,
        [SMEM, SMEM, VMEM],
        [SMEM] * 2 + [VMEM] * PLANES,
        [],
        nbytes=3 << 20,
    )(rank, target, gradients[0])
    summands = [terms[0]] + [settle(along(terms[k], k), SUM_HINT) for k in (1, 3, 2)]
    part = like((8, 256, 128))
    *halves, table = call(
        root_halves,
        "root_halves",
        [part] * 4 + [like((8,), jnp.int32)],
        [SMEM, VMEM, VMEM],
        [VMEM] * 4 + [SMEM],
        [pltpu.SMEM((PLANES,), jnp.int32)],
    )(sorted_target, root_left, root_right)
    halves = [*halves[:2], *(across(x) for x in halves[2:])]
    roots = call(
        roots_by_plane,
        "roots_by_plane",
        [part] * PLANES,
        [SMEM] + [VMEM] * 4,
        [VMEM] * PLANES,
        [],
    )(table, *halves)

    outgoing = call(
        sum_and_place,
        "sum_and_place",
        like((fsdp_count, rows, width // CORES)),
        [SMEM, ANY] + [VMEM] * PLANES,
        VMEM,
        [],
        nbytes=3 << 20,
    )(sorted_target, roots[0], *summands)
    roots, _ = lax.optimization_barrier((roots, outgoing))
    first = settle(along(roots[2], 2), ROOT_HINT)
    arrived = lax.all_to_all(outgoing, "fsdp", split_axis=0, concat_axis=0, tiled=True)

    roots = [roots[0], along(roots[1], 1), first, along(roots[3], 3)]
    l_own, r_cols = call(
        collect,
        "collect",
        [like((width, 512))] * 2,
        [VMEM] * PLANES,
        [VMEM] * 2,
        [],
    )(*roots)

    arrived, l_far = together(arrived, across(l_own))
    s_own = arrived.reshape(width, width // CORES)
    s_far = across(s_own)
    grams = call(
        gram,
        "gram",
        [like((2, 256, 512))] * PLANES,
        [VMEM] * 2,
        [VMEM] * PLANES,
        [],
        flops=4 * 1024 * 1024 * 512,
        nbytes=4 << 20,
    )(s_own, s_far)
    update = call(
        update_block,
        "update_block",
        like((PLANES, fsdp_count, rows, 128)),
        [VMEM] * 5,
        VMEM,
        [pltpu.VMEM((width, 512), BF16)],
        flops=4 * 1024 * 1024 * 512,
        nbytes=6 << 20,
    )(s_own, s_far, l_own, l_far, r_cols)
    update = update.reshape(PLANES * fsdp_count, rows, 128)
    returned = lax.all_to_all(update, ("replica", "fsdp"), split_axis=0, concat_axis=0, tiled=True)
    new = call(
        pick,
        "pick",
        like((blocks, rows, width // PLANES)),
        [SMEM, SMEM, VMEM],
        VMEM,
        [],
        nbytes=2 << 20,
    )(order, sorted_target, returned.reshape(PLANES, fsdp_count // CORES, CORES, rows, 128))

    first = settle(along(grams[2], 2), GRAM_HINT)
    grams = [grams[0], along(grams[1], 1), first, along(grams[3], 3)]
    grams_far = [across(x) for x in grams]
    stat_left, stat_right = call(
        preload,
        "preload",
        [like(stat_left.shape, F32), like(stat_right.shape, F32)],
        [ANY] * 3,
        [VMEM] * 2,
        [pltpu.SemaphoreType.DMA((2,))],
    )(first, stat_left, stat_right)
    left_new, right_new = call(
        statistics,
        "statistics",
        [like(stat_left.shape, F32)] * 2,
        [SMEM, VMEM, VMEM] + [ANY] * (2 * PLANES),
        [ANY] * 2,
        [
            pltpu.VMEM((SLOTS, 2, 256, width), BF16),
            pltpu.VMEM((SLOTS, 2, 256, width), F32),
            pltpu.SemaphoreType.DMA((SLOTS,)),
            pltpu.SemaphoreType.DMA((2 * SLOTS,)),
        ],
        nbytes=8 << 20,
    )(table, stat_left, stat_right, *grams, *grams_far)

    return (left_new, right_new, new)


def solution(mesh):
    placed = (
        P("replica", None, "fsdp", None),
        P("fsdp", "replica", None),
        P("fsdp", "replica", None),
        P("fsdp", "replica", None),
        P("fsdp", None, "replica"),
        P(),
        P(),
    )
    return jax.shard_map(
        per_device,
        mesh=mesh,
        in_specs=placed,
        out_specs=(
            P("fsdp", "replica", None),
            P("fsdp", "replica", None),
            P(None, "fsdp", "replica"),
        ),
        check_vma=False,
    )
```

```python
import functools

import jax
import jax.numpy as jnp
from jax import lax
from jax.experimental import pallas as pl
from jax.experimental.pallas import tpu as pltpu
from jax.sharding import PartitionSpec as P

PLANES = 4
CORES = 2
SLOTS = 2
VMEM_LIMIT = 12 * 1024 * 1024
VMEM_WHOLE = 60 * 1024 * 1024
SUM_HINT = 20 * 1000**3
ROOT_HINT = 20 * 1000**3
GRAM_HINT = 20 * 1000**3
F32 = jnp.float32
BF16 = jnp.bfloat16
ANY = pl.BlockSpec(memory_space=pl.ANY)
VMEM = pl.BlockSpec(memory_space=pltpu.VMEM)
SMEM = pl.BlockSpec(memory_space=pltpu.SMEM)


def call(body, name, out_shape, in_specs, out_specs, scratch, flops=0, nbytes=0, vmem=VMEM_LIMIT):
    return pl.pallas_call(
        body,
        name=name,
        out_shape=out_shape,
        in_specs=in_specs,
        out_specs=out_specs,
        scratch_shapes=scratch,
        compiler_params=pltpu.CompilerParams(vmem_limit_bytes=vmem),
        cost_estimate=pl.CostEstimate(flops=flops, bytes_accessed=nbytes, transcendentals=0),
    )


def like(shape, dtype=BF16):
    return jax.ShapeDtypeStruct(shape, dtype)


def my_place():
    f = lax.axis_index("fsdp")
    return lax.axis_index("replica"), f // CORES, f % CORES


def by_plane(rank, target, g, sorted_target, order, *outs):
    count = g.shape[0]
    r, _, _ = my_place()

    @pl.loop(0, count, unroll=8)
    def _(b):
        order[rank[b]] = b
        sorted_target[rank[b]] = target[b]

    for k in range(PLANES):
        plane = (r + k) % PLANES
        for j in range(count // PLANES):
            outs[k][j] = g[order[PLANES * j + plane]]


def sum_and_place(sorted_target, _, own, one, two, three, out):
    r, _, _ = my_place()
    out[...] = jnp.zeros_like(out)
    for j in range(own.shape[0]):
        chip = sorted_target[PLANES * j + r] // (CORES * SLOTS)
        total = own[j].astype(F32) + one[j].astype(F32) + two[j].astype(F32) + three[j].astype(F32)
        out[chip] = total.astype(BF16)


def root_halves(sorted_target, left, right, *outs):
    *outs, table, slots = outs
    r, q, c = my_place()
    for i in range(8):
        table[i] = 0
    for plane in range(PLANES):
        slots[plane] = SLOTS * c

    @pl.loop(0, sorted_target.shape[0], unroll=8)
    def _(i):
        t = sorted_target[i]

        @pl.when(t // (CORES * SLOTS) == q)
        def _():
            slots[i % PLANES] = t % (CORES * SLOTS)

        @pl.when(t // SLOTS == CORES * q + c)
        def _():
            table[4 + t % SLOTS] = i % PLANES
            table[6 + t % SLOTS] = 1

    for k in range(PLANES):
        local = slots[(r + k) % PLANES]
        table[k] = jnp.where(local // SLOTS == c, 0, SLOTS) + local % SLOTS
    for i, which in enumerate((c, 1 - c)):
        for s in range(SLOTS):
            out = outs[SLOTS * i + s]
            for m in range(4):
                first = pl.multiple_of(which * 512 + 128 * m, 128)
                out[m] = left[s, :, pl.ds(first, 128)]
                first = pl.multiple_of(which * 128, 128)
                out[4 + m] = right[s, 256 * m : 256 * (m + 1), pl.ds(first, 128)]


def roots_by_plane(table, *refs):
    ins, outs = refs[:4], refs[4:]
    for k in (2, 1, 3, 0):
        for i in range(2 * SLOTS):

            @pl.when(table[k] == i)
            def _():
                outs[k][...] = ins[i][...]


def collect(*refs):
    roots, (left, right) = refs[:PLANES], refs[PLANES:]
    for k in range(PLANES):
        for m in range(4):
            left[256 * k : 256 * (k + 1), 128 * m : 128 * (m + 1)] = roots[k][m]
            right[256 * m : 256 * (m + 1), 128 * k : 128 * (k + 1)] = roots[k][4 + m]


def settle(x, flops):
    return pl.pallas_call(
        lambda *_: None,
        name="settle",
        out_shape=like(x.shape),
        in_specs=[VMEM],
        out_specs=VMEM,
        input_output_aliases={0: 0},
        compiler_params=pltpu.CompilerParams(vmem_limit_bytes=VMEM_LIMIT),
        cost_estimate=pl.CostEstimate(flops=flops, bytes_accessed=0, transcendentals=0),
    )(x)


def together(x, y):
    return pl.pallas_call(
        lambda *_: None,
        name="together",
        out_shape=[like(x.shape), like(y.shape)],
        in_specs=[VMEM] * 2,
        out_specs=[VMEM] * 2,
        input_output_aliases={0: 0, 1: 1},
        compiler_params=pltpu.CompilerParams(vmem_limit_bytes=VMEM_LIMIT),
    )(x, y)


def gram(s_own, s_far, *outs):
    grams, block = outs[:PLANES], outs[PLANES]
    r, _, c = my_place()
    for i in range(s_own.shape[0]):
        block[pl.ds(pl.multiple_of(32 * i + 16 * c, 16), 16), :] = s_own[i]
        block[pl.ds(pl.multiple_of(32 * i + 16 * (1 - c), 16), 16), :] = s_far[i]
    near = pl.ds(pl.multiple_of(c * 512, 512), 512)
    across_rows = (((1,), (1,)), ((), ()))
    across_columns = (((0,), (0,)), ((), ()))
    for k in range(PLANES):
        plane = (r + k) % PLANES
        strip = pl.ds(pl.multiple_of(plane * 256, 256), 256)
        left = lax.dot_general(block[strip, :], block[near, :], across_rows, preferred_element_type=F32)
        grams[k][0] = (left / 1024).astype(BF16)
        right = lax.dot_general(block[:, strip], block[:, near], across_columns, preferred_element_type=F32)
        grams[k][1] = (right / 1024).astype(BF16)


def update_block(block, l_own, l_far, r_cols, out, half):
    r, _, c = my_place()
    near = pl.ds(pl.multiple_of(c * 512, 512), 512)
    far = pl.ds(pl.multiple_of((1 - c) * 512, 512), 512)
    for m in range(4):
        rows = slice(256 * m, 256 * (m + 1))
        total = jnp.dot(block[rows, :], r_cols[...], preferred_element_type=F32)
        half[rows, :] = total.astype(BF16)
    for k in range(PLANES):
        rows = slice(256 * k, 256 * (k + 1))
        source = (r - k + PLANES) % PLANES
        total = jnp.dot(l_own[rows, :], half[near, :], preferred_element_type=F32)
        total += jnp.dot(l_far[rows, :], half[far, :], preferred_element_type=F32)
        total = total.astype(BF16)
        for kk in range(PLANES):
            plane = (r - kk + PLANES) % PLANES
            part = total[:, 128 * kk : 128 * (kk + 1)].reshape(16, 16, 128)
            out[plane, pl.ds(16 * source, 16)] = part


def preload(_, stat_left, stat_right, left, right, sems):
    copies = [pltpu.make_async_copy(stat_left, left, sems.at[0])]
    copies.append(pltpu.make_async_copy(stat_right, right, sems.at[1]))
    for copy in copies:
        copy.start()
    for copy in copies:
        copy.wait()


def statistics(table, left, right, *rest):
    own, other, (left_new, right_new), scratch = rest[:4], rest[4:8], rest[8:10], rest[10:]
    added, sums, g_sems, out_sems = scratch
    r, _, c = my_place()
    pairs = ((left, left_new), (right, right_new))
    near = pl.ds(pl.multiple_of(c * 512, 512), 512)
    far = pl.ds(pl.multiple_of((1 - c) * 512, 512), 512)
    for s in range(SLOTS):
        step = (r - table[4 + s] + PLANES) % PLANES
        for k in range(PLANES):

            @pl.when(step == k)
            def _():
                pltpu.make_async_copy(own[k], added.at[s, :, :, near], g_sems.at[s]).start()
                pltpu.make_async_copy(other[k], added.at[s, :, :, far], g_sems.at[s]).start()

    stores = []
    for s in range(SLOTS):
        pltpu.make_async_copy(added.at[s], added.at[s], g_sems.at[s]).wait()
        used = table[6 + s] > 0
        for i, (here, out) in enumerate(pairs):
            sums[s, i] = jnp.where(used, here[s] + added[s, i].astype(F32), here[s])
            store = pltpu.make_async_copy(sums.at[s, i], out.at[s], out_sems.at[2 * s + i])
            store.start()
            stores.append(store)
    for store in stores:
        store.wait()


def pick(order, sorted_target, received, out):
    for i in range(out.shape[0]):
        chip = sorted_target[i] // (CORES * SLOTS)
        for h in range(CORES):
            out[order[i], :, 128 * h : 128 * (h + 1)] = received[i % PLANES, chip, h]


def per_device(gradients, stat_left, stat_right, root_left, root_right, block_owner, block_slot):
    blocks, rows, width = gradients.shape[1:]
    each = blocks // PLANES
    fsdp_count = lax.axis_size("fsdp")
    target = block_owner * SLOTS + block_slot
    rank = jnp.sum((target[None, :] < target[:, None]).astype(jnp.int32), axis=1)

    def along(x, step):
        return lax.ppermute(x, "replica", [(i, (i + step) % PLANES) for i in range(PLANES)])

    def across(x):
        return lax.ppermute(x, "fsdp", [(i, i ^ 1) for i in range(fsdp_count)])

    sorted_target, order, *terms = call(
        by_plane,
        "by_plane",
        [like((blocks,), jnp.int32)] * 2 + [like((each, rows, width))] * PLANES,
        [SMEM, SMEM, VMEM],
        [SMEM] * 2 + [VMEM] * PLANES,
        [],
        nbytes=3 << 20,
    )(rank, target, gradients[0])
    summands = [terms[0]] + [settle(along(terms[k], k), SUM_HINT) for k in (1, 3, 2)]
    part = like((8, 256, 128))
    *halves, table = call(
        root_halves,
        "root_halves",
        [part] * 4 + [like((8,), jnp.int32)],
        [SMEM, VMEM, VMEM],
        [VMEM] * 4 + [SMEM],
        [pltpu.SMEM((PLANES,), jnp.int32)],
    )(sorted_target, root_left, root_right)
    halves = [*halves[:2], *(across(x) for x in halves[2:])]
    roots = call(
        roots_by_plane,
        "roots_by_plane",
        [part] * PLANES,
        [SMEM] + [VMEM] * 4,
        [VMEM] * PLANES,
        [],
    )(table, *halves)

    outgoing = call(
        sum_and_place,
        "sum_and_place",
        like((fsdp_count // CORES, rows, width)),
        [SMEM, ANY] + [VMEM] * PLANES,
        VMEM,
        [],
        nbytes=3 << 20,
    )(sorted_target, roots[0], *summands)
    roots, _ = lax.optimization_barrier((roots, outgoing))
    first = settle(along(roots[2], 2), ROOT_HINT)
    same_core = [list(range(c, fsdp_count, CORES)) for c in range(CORES)]
    arrived = lax.all_to_all(
        outgoing, "fsdp", split_axis=0, concat_axis=0, tiled=True, axis_index_groups=same_core
    )

    roots = [roots[0], along(roots[1], 1), first, along(roots[3], 3)]
    l_own, r_cols = call(
        collect,
        "collect",
        [like((width, 512))] * 2,
        [VMEM] * PLANES,
        [VMEM] * 2,
        [],
    )(*roots)

    arrived, l_far = together(arrived, across(l_own))
    s_own = arrived
    s_far = across(s_own)
    *grams, block = call(
        gram,
        "gram",
        [like((2, 256, 512))] * PLANES + [like((width, width))],
        [VMEM] * 2,
        [VMEM] * (PLANES + 1),
        [],
        flops=4 * 1024 * 1024 * 512,
        nbytes=4 << 20,
    )(s_own, s_far)
    update = call(
        update_block,
        "update_block",
        like((PLANES, fsdp_count, rows, 128)),
        [VMEM] * 4,
        VMEM,
        [pltpu.VMEM((width, 512), BF16)],
        flops=4 * 1024 * 1024 * 512,
        nbytes=6 << 20,
    )(block, l_own, l_far, r_cols)
    update = update.reshape(PLANES * fsdp_count, rows, 128)
    returned = lax.all_to_all(update, ("replica", "fsdp"), split_axis=0, concat_axis=0, tiled=True)
    new = call(
        pick,
        "pick",
        like((blocks, rows, width // PLANES)),
        [SMEM, SMEM, VMEM],
        VMEM,
        [],
        nbytes=2 << 20,
    )(order, sorted_target, returned.reshape(PLANES, fsdp_count // CORES, CORES, rows, 128))

    first = settle(along(grams[2], 2), GRAM_HINT)
    grams = [grams[0], along(grams[1], 1), first, along(grams[3], 3)]
    grams_far = [across(x) for x in grams]
    stat_left, stat_right = call(
        preload,
        "preload",
        [like(stat_left.shape, F32), like(stat_right.shape, F32)],
        [ANY] * 3,
        [VMEM] * 2,
        [pltpu.SemaphoreType.DMA((2,))],
    )(first, stat_left, stat_right)
    left_new, right_new = call(
        statistics,
        "statistics",
        [like(stat_left.shape, F32)] * 2,
        [SMEM, VMEM, VMEM] + [ANY] * (2 * PLANES),
        [ANY] * 2,
        [
            pltpu.VMEM((SLOTS, 2, 256, width), BF16),
            pltpu.VMEM((SLOTS, 2, 256, width), F32),
            pltpu.SemaphoreType.DMA((SLOTS,)),
            pltpu.SemaphoreType.DMA((2 * SLOTS,)),
        ],
        nbytes=8 << 20,
    )(table, stat_left, stat_right, *grams, *grams_far)

    return (left_new, right_new, new)


def solution(mesh):
    placed = (
        P("replica", None, "fsdp", None),
        P("fsdp", "replica", None),
        P("fsdp", "replica", None),
        P("fsdp", "replica", None),
        P("fsdp", None, "replica"),
        P(),
        P(),
    )
    return jax.shard_map(
        per_device,
        mesh=mesh,
        in_specs=placed,
        out_specs=(
            P("fsdp", "replica", None),
            P("fsdp", "replica", None),
            P(None, "fsdp", "replica"),
        ),
        check_vma=False,
    )
```

```python
import functools

import jax
import jax.numpy as jnp
from jax import lax
from jax.experimental import pallas as pl
from jax.experimental.pallas import tpu as pltpu
from jax.sharding import PartitionSpec as P

PLANES = 4
CORES = 2
SLOTS = 2
VMEM_LIMIT = 12 * 1024 * 1024
VMEM_WHOLE = 60 * 1024 * 1024
SUM_HINT = 20 * 1000**3
ROOT_HINT = 20 * 1000**3
GRAM_HINT = 20 * 1000**3
F32 = jnp.float32
BF16 = jnp.bfloat16
ANY = pl.BlockSpec(memory_space=pl.ANY)
VMEM = pl.BlockSpec(memory_space=pltpu.VMEM)
SMEM = pl.BlockSpec(memory_space=pltpu.SMEM)


def call(body, name, out_shape, in_specs, out_specs, scratch, flops=0, nbytes=0, vmem=VMEM_LIMIT):
    return pl.pallas_call(
        body,
        name=name,
        out_shape=out_shape,
        in_specs=in_specs,
        out_specs=out_specs,
        scratch_shapes=scratch,
        compiler_params=pltpu.CompilerParams(vmem_limit_bytes=vmem),
        cost_estimate=pl.CostEstimate(flops=flops, bytes_accessed=nbytes, transcendentals=0),
    )


def like(shape, dtype=BF16):
    return jax.ShapeDtypeStruct(shape, dtype)


def my_place():
    f = lax.axis_index("fsdp")
    return lax.axis_index("replica"), f // CORES, f % CORES


def slots_of(owner, slot, target):
    target[...] = owner[...] * SLOTS + slot[...]


def by_plane(rank, target, g, sorted_target, order, *outs):
    count = g.shape[0]
    r, _, _ = my_place()

    @pl.loop(0, count, unroll=8)
    def _(b):
        order[rank[b]] = b
        sorted_target[rank[b]] = target[b]

    for k in range(PLANES):
        plane = (r + k) % PLANES
        for j in range(count // PLANES):
            outs[k][j] = g[order[PLANES * j + plane]]


def sum_and_place(sorted_target, _, own, one, two, three, out):
    r, _, _ = my_place()
    out[...] = jnp.zeros_like(out)
    for j in range(own.shape[0]):
        chip = sorted_target[PLANES * j + r] // (CORES * SLOTS)
        total = own[j].astype(F32) + one[j].astype(F32) + two[j].astype(F32) + three[j].astype(F32)
        out[chip] = total.astype(BF16)


def root_halves(sorted_target, left, right, *outs):
    *outs, table, slots = outs
    r, q, c = my_place()
    for i in range(8):
        table[i] = 0
    for plane in range(PLANES):
        slots[plane] = SLOTS * c

    @pl.loop(0, sorted_target.shape[0], unroll=8)
    def _(i):
        t = sorted_target[i]

        @pl.when(t // (CORES * SLOTS) == q)
        def _():
            slots[i % PLANES] = t % (CORES * SLOTS)

        @pl.when(t // SLOTS == CORES * q + c)
        def _():
            table[4 + t % SLOTS] = i % PLANES
            table[6 + t % SLOTS] = 1

    for k in range(PLANES):
        local = slots[(r + k) % PLANES]
        table[k] = jnp.where(local // SLOTS == c, 0, SLOTS) + local % SLOTS
    for i, which in enumerate((c, 1 - c)):
        for s in range(SLOTS):
            out = outs[SLOTS * i + s]
            for m in range(4):
                first = pl.multiple_of(which * 512 + 128 * m, 128)
                out[m] = left[s, :, pl.ds(first, 128)]
                first = pl.multiple_of(which * 128, 128)
                out[4 + m] = right[s, 256 * m : 256 * (m + 1), pl.ds(first, 128)]


def roots_by_plane(table, *refs):
    ins, outs = refs[:4], refs[4:]
    for k in (2, 1, 3, 0):
        for i in range(2 * SLOTS):

            @pl.when(table[k] == i)
            def _():
                outs[k][...] = ins[i][...]


def collect(*refs):
    roots, (left, right) = refs[:PLANES], refs[PLANES:]
    for k in range(PLANES):
        for m in range(4):
            left[256 * k : 256 * (k + 1), 128 * m : 128 * (m + 1)] = roots[k][m]
            right[256 * m : 256 * (m + 1), 128 * k : 128 * (k + 1)] = roots[k][4 + m]


def settle(x, flops):
    return pl.pallas_call(
        lambda *_: None,
        name="settle",
        out_shape=like(x.shape),
        in_specs=[VMEM],
        out_specs=VMEM,
        input_output_aliases={0: 0},
        compiler_params=pltpu.CompilerParams(vmem_limit_bytes=VMEM_LIMIT),
        cost_estimate=pl.CostEstimate(flops=flops, bytes_accessed=0, transcendentals=0),
    )(x)


def together(x, y):
    return pl.pallas_call(
        lambda *_: None,
        name="together",
        out_shape=[like(x.shape), like(y.shape)],
        in_specs=[VMEM] * 2,
        out_specs=[VMEM] * 2,
        input_output_aliases={0: 0, 1: 1},
        compiler_params=pltpu.CompilerParams(vmem_limit_bytes=VMEM_LIMIT),
    )(x, y)


def gram(s_own, s_far, *outs):
    grams, block = outs[:PLANES], outs[PLANES]
    r, _, c = my_place()
    for i in range(s_own.shape[0]):
        block[pl.ds(pl.multiple_of(32 * i + 16 * c, 16), 16), :] = s_own[i]
        block[pl.ds(pl.multiple_of(32 * i + 16 * (1 - c), 16), 16), :] = s_far[i]
    near = pl.ds(pl.multiple_of(c * 512, 512), 512)
    across_rows = (((1,), (1,)), ((), ()))
    across_columns = (((0,), (0,)), ((), ()))
    for k in range(PLANES):
        plane = (r + k) % PLANES
        strip = pl.ds(pl.multiple_of(plane * 256, 256), 256)
        left = lax.dot_general(block[strip, :], block[near, :], across_rows, preferred_element_type=F32)
        grams[k][0] = (left / 1024).astype(BF16)
        right = lax.dot_general(block[:, strip], block[:, near], across_columns, preferred_element_type=F32)
        grams[k][1] = (right / 1024).astype(BF16)


def update_block(block, l_own, l_far, r_cols, out, half):
    r, _, c = my_place()
    near = pl.ds(pl.multiple_of(c * 512, 512), 512)
    far = pl.ds(pl.multiple_of((1 - c) * 512, 512), 512)
    for m in range(4):
        rows = slice(256 * m, 256 * (m + 1))
        total = jnp.dot(block[rows, :], r_cols[...], preferred_element_type=F32)
        half[rows, :] = total.astype(BF16)
    for k in range(PLANES):
        rows = slice(256 * k, 256 * (k + 1))
        source = (r - k + PLANES) % PLANES
        total = jnp.dot(l_own[rows, :], half[near, :], preferred_element_type=F32)
        total += jnp.dot(l_far[rows, :], half[far, :], preferred_element_type=F32)
        total = total.astype(BF16)
        for kk in range(PLANES):
            plane = (r - kk + PLANES) % PLANES
            part = total[:, 128 * kk : 128 * (kk + 1)].reshape(16, 16, 128)
            out[plane, pl.ds(16 * source, 16)] = part


def preload(_, stat_left, stat_right, left, right, sems):
    copies = [pltpu.make_async_copy(stat_left, left, sems.at[0])]
    copies.append(pltpu.make_async_copy(stat_right, right, sems.at[1]))
    for copy in copies:
        copy.start()
    for copy in copies:
        copy.wait()


def statistics(table, left, right, *rest):
    own, other, (left_new, right_new), scratch = rest[:4], rest[4:8], rest[8:10], rest[10:]
    added, sums, g_sems, out_sems = scratch
    r, _, c = my_place()
    pairs = ((left, left_new), (right, right_new))
    near = pl.ds(pl.multiple_of(c * 512, 512), 512)
    far = pl.ds(pl.multiple_of((1 - c) * 512, 512), 512)
    for s in range(SLOTS):
        step = (r - table[4 + s] + PLANES) % PLANES
        for k in range(PLANES):

            @pl.when(step == k)
            def _():
                pltpu.make_async_copy(own[k], added.at[s, :, :, near], g_sems.at[s]).start()
                pltpu.make_async_copy(other[k], added.at[s, :, :, far], g_sems.at[s]).start()

    stores = []
    for s in range(SLOTS):
        pltpu.make_async_copy(added.at[s], added.at[s], g_sems.at[s]).wait()
        used = table[6 + s] > 0
        for i, (here, out) in enumerate(pairs):
            sums[s, i] = jnp.where(used, here[s] + added[s, i].astype(F32), here[s])
            store = pltpu.make_async_copy(sums.at[s, i], out.at[s], out_sems.at[2 * s + i])
            store.start()
            stores.append(store)
    for store in stores:
        store.wait()


def pick(order, sorted_target, received, out):
    for i in range(out.shape[0]):
        chip = sorted_target[i] // (CORES * SLOTS)
        for h in range(CORES):
            out[order[i], :, 128 * h : 128 * (h + 1)] = received[i % PLANES, chip, h]


def per_device(gradients, stat_left, stat_right, root_left, root_right, block_owner, block_slot):
    blocks, rows, width = gradients.shape[1:]
    each = blocks // PLANES
    fsdp_count = lax.axis_size("fsdp")
    target = call(
        slots_of,
        "slots_of",
        like(block_owner.shape, jnp.int32),
        [VMEM] * 2,
        VMEM,
        [],
        flops=SUM_HINT,
    )(block_owner, block_slot)
    rank = jnp.sum((target[None, :] < target[:, None]).astype(jnp.int32), axis=1)

    def along(x, step):
        return lax.ppermute(x, "replica", [(i, (i + step) % PLANES) for i in range(PLANES)])

    def across(x):
        return lax.ppermute(x, "fsdp", [(i, i ^ 1) for i in range(fsdp_count)])

    sorted_target, order, *terms = call(
        by_plane,
        "by_plane",
        [like((blocks,), jnp.int32)] * 2 + [like((each, rows, width))] * PLANES,
        [SMEM, SMEM, VMEM],
        [SMEM] * 2 + [VMEM] * PLANES,
        [],
        nbytes=3 << 20,
    )(rank, target, gradients[0])
    summands = [terms[0]] + [settle(along(terms[k], k), SUM_HINT) for k in (1, 3, 2)]
    part = like((8, 256, 128))
    *halves, table = call(
        root_halves,
        "root_halves",
        [part] * 4 + [like((8,), jnp.int32)],
        [SMEM, VMEM, VMEM],
        [VMEM] * 4 + [SMEM],
        [pltpu.SMEM((PLANES,), jnp.int32)],
    )(sorted_target, root_left, root_right)
    halves = [*halves[:2], *(across(x) for x in halves[2:])]
    roots = call(
        roots_by_plane,
        "roots_by_plane",
        [part] * PLANES,
        [SMEM] + [VMEM] * 4,
        [VMEM] * PLANES,
        [],
    )(table, *halves)

    outgoing = call(
        sum_and_place,
        "sum_and_place",
        like((fsdp_count // CORES, rows, width)),
        [SMEM, ANY] + [VMEM] * PLANES,
        VMEM,
        [],
        nbytes=3 << 20,
    )(sorted_target, roots[0], *summands)
    roots, _ = lax.optimization_barrier((roots, outgoing))
    first = settle(along(roots[2], 2), ROOT_HINT)
    same_core = [list(range(c, fsdp_count, CORES)) for c in range(CORES)]
    arrived = lax.all_to_all(
        outgoing, "fsdp", split_axis=0, concat_axis=0, tiled=True, axis_index_groups=same_core
    )

    roots = [roots[0], along(roots[1], 1), first, along(roots[3], 3)]
    l_own, r_cols = call(
        collect,
        "collect",
        [like((width, 512))] * 2,
        [VMEM] * PLANES,
        [VMEM] * 2,
        [],
    )(*roots)

    arrived, l_far = together(arrived, across(l_own))
    s_own = arrived
    s_far = across(s_own)
    *grams, block = call(
        gram,
        "gram",
        [like((2, 256, 512))] * PLANES + [like((width, width))],
        [VMEM] * 2,
        [VMEM] * (PLANES + 1),
        [],
        flops=4 * 1024 * 1024 * 512,
        nbytes=4 << 20,
    )(s_own, s_far)
    update = call(
        update_block,
        "update_block",
        like((PLANES, fsdp_count, rows, 128)),
        [VMEM] * 4,
        VMEM,
        [pltpu.VMEM((width, 512), BF16)],
        flops=4 * 1024 * 1024 * 512,
        nbytes=6 << 20,
    )(block, l_own, l_far, r_cols)
    update = update.reshape(PLANES * fsdp_count, rows, 128)
    returned = lax.all_to_all(update, ("replica", "fsdp"), split_axis=0, concat_axis=0, tiled=True)
    new = call(
        pick,
        "pick",
        like((blocks, rows, width // PLANES)),
        [SMEM, SMEM, VMEM],
        VMEM,
        [],
        nbytes=2 << 20,
    )(order, sorted_target, returned.reshape(PLANES, fsdp_count // CORES, CORES, rows, 128))

    first = settle(along(grams[2], 2), GRAM_HINT)
    grams = [grams[0], along(grams[1], 1), first, along(grams[3], 3)]
    grams_far = [across(x) for x in grams]
    stat_left, stat_right = call(
        preload,
        "preload",
        [like(stat_left.shape, F32), like(stat_right.shape, F32)],
        [ANY] * 3,
        [VMEM] * 2,
        [pltpu.SemaphoreType.DMA((2,))],
    )(first, stat_left, stat_right)
    left_new, right_new = call(
        statistics,
        "statistics",
        [like(stat_left.shape, F32)] * 2,
        [SMEM, VMEM, VMEM] + [ANY] * (2 * PLANES),
        [ANY] * 2,
        [
            pltpu.VMEM((SLOTS, 2, 256, width), BF16),
            pltpu.VMEM((SLOTS, 2, 256, width), F32),
            pltpu.SemaphoreType.DMA((SLOTS,)),
            pltpu.SemaphoreType.DMA((2 * SLOTS,)),
        ],
        nbytes=8 << 20,
    )(table, stat_left, stat_right, *grams, *grams_far)

    return (left_new, right_new, new)


def solution(mesh):
    placed = (
        P("replica", None, "fsdp", None),
        P("fsdp", "replica", None),
        P("fsdp", "replica", None),
        P("fsdp", "replica", None),
        P("fsdp", None, "replica"),
        P(),
        P(),
    )
    return jax.shard_map(
        per_device,
        mesh=mesh,
        in_specs=placed,
        out_specs=(
            P("fsdp", "replica", None),
            P("fsdp", "replica", None),
            P(None, "fsdp", "replica"),
        ),
        check_vma=False,
    )
```
